32 devices in a mesh: replica: 2 (over y), pool: 4 (over z), tensor: 2 (over x), seq: 2 (over core).
Axes of the slice: x: 2, y: 2, z: 4, core: 2. Of those that a mesh axis runs over, the one named last changes fastest.
Arguments:
- queries: bfloat16 [8, 256, 32, 128], P(('replica', 'pool'), 'seq', 'tensor'), parts along dimension 0
- suffix_kv: bfloat16 [8, 2, 256, 8, 128], P(('replica', 'pool'), None, 'seq', 'tensor'), parts along dimension 0
- page_store: bfloat16 [256, 2, 8, 128, 128], P(('replica', 'pool'), None, ('tensor', 'seq')), parts along dimension 0
- holder_table: int32 [8, 8, 2], P('replica'), parts along dimension 0, may hold values from 0 to 31, as said below
- prefix_pages: int32 [8], P('replica'), parts along dimension 0, may hold values from 1 to 8, 20 in all
- suffix_pages: int32 [8], P('replica'), parts along dimension 0, may hold values from 1 to 2, 6 in all
- fresh_alloc: int32 [8, 2, 2], P('replica'), parts along dimension 0, may hold values from 0 to 3, as said below
Outputs:
- attention: bfloat16 [8, 256, 32, 128], P(('replica', 'pool'), 'seq', 'tensor'), parts along dimension 0
- row_lse: float32 [8, 32, 256], P(('replica', 'pool'), 'tensor', 'seq'), parts along dimension 0
- fresh_store: bfloat16 [16, 2, 8, 128, 128], P(('replica', 'pool'), None, ('tensor', 'seq')), parts along dimension 0
The draws below stay inside these ranges and needn't reach their ends.
There are 2 independent parts, one for each index of `replica`. The reference program is written for one: setup_inputs(seed, part) draws one part's arguments, and reference() takes and returns one part's arrays. A program takes and returns all parts, laid end to end along the dimension named above; each array names one. Nothing has to cross between parts.
Inputs may be any that keep to these rules, and one draw needn't show every extreme that they name: `holder_table`: entry [r, p, 0] is a holder below 4 and entry [r, p, 1] a slot below 32. Over the 8 entries of one request each holder is named exactly 2 times, so a request with 8 prefix pages takes 2 pages from every holder. `fresh_alloc`: entry [r, q] holds a holder below 4 and the slot q; every pair of holder and slot below 2 is named by exactly one entry, and the 2 pages of one request go to 2 different holders. `prefix_pages`: some request has 8 prefix pages. `suffix_pages`: some request has 2 suffix pages.
All inputs are finite; a program needn't handle non-finite values.
Results may differ from the reference program's by a relative error of at most 0.0051.
Values may be sent and summed in bfloat16 or wider, within the bound.
A program may use at most 64 MiB of HBM per device.

```python
import math
import jax
import jax.numpy as jnp
import numpy as np
from jax import lax

QH = 32
KVH = 8
HD = 128
PAGE = 128
REQS = 4
PMAX = 8
SLOTS = 32
SPAGES = 2
FRESH = 2
SUF = 256
N_POOL = 4


def draw_queries(key, part):
    key = jax.random.fold_in(key, 2)
    shape_all = (REQS, SUF, QH, HD)
    base_draw = jax.random.truncated_normal(key, -5.0, 5.0, shape_all, jnp.float32) * 1.5
    return base_draw.astype(jnp.bfloat16)


def draw_suffix_kv(key, part):
    key = jax.random.fold_in(key, 3)
    shape_all = (REQS, 2, SUF, KVH, HD)
    factor = jnp.array([1.0, 4.0], jnp.float32)[None, :, None, None, None]
    base_draw = jax.random.truncated_normal(key, -4.0, 4.0, shape_all, jnp.float32) * factor
    return base_draw.astype(jnp.bfloat16)


def draw_page_store(key, part):
    key = jax.random.fold_in(key, 1)
    shape_all = (N_POOL * SLOTS, 2, KVH, PAGE, HD)
    factor = jnp.array([1.0, 4.0], jnp.float32)[None, :, None, None, None]
    base_draw = jax.random.truncated_normal(key, -4.0, 4.0, shape_all, jnp.float32)
    return (base_draw * factor).astype(jnp.bfloat16)


def draw_holder_table(key, part):
    key = jax.random.fold_in(key, 4)
    key_perm, key_slot = jax.random.split(key)
    row_keys = jax.random.split(key_perm, REQS)
    orders = jax.vmap(lambda row_key: jax.random.permutation(row_key, PMAX))(row_keys)
    holders = (orders % N_POOL).astype(jnp.int32)
    slot_ids = jax.random.randint(key_slot, (REQS, PMAX), 0, SLOTS).astype(jnp.int32)
    return jnp.stack([holders, slot_ids], axis=-1)


def draw_fresh_alloc(key, part):
    key = jax.random.fold_in(key, 5)
    key_perm, key_step = jax.random.split(key)
    orders = jax.random.permutation(key_perm, REQS).astype(jnp.int32)
    stride = jax.random.randint(key_step, (), 0, N_POOL // SPAGES).astype(jnp.int32) * SPAGES + 1
    stride = jnp.where(N_POOL // SPAGES > 1, stride, jnp.int32(1))
    page_ids = jnp.arange(SPAGES, dtype=jnp.int32)
    holders = (orders[:, None] + page_ids[None, :] * stride) % N_POOL
    slot_ids = jnp.broadcast_to(page_ids[None, :], (REQS, SPAGES))
    return jnp.stack([holders, slot_ids], axis=-1).astype(jnp.int32)


def profile(number_of, total, limit, skew):
    loads = [(1 << 20) // math.isqrt(grade ** skew) + 1 for grade in range(2, number_of + 1)]
    spare, given = total - limit - (number_of - 1), [1] * (number_of - 1)
    while spare > 0:
        free = [i for i in range(number_of - 1) if given[i] < limit]
        mass, budget = sum([loads[i] for i in free]), spare
        for i in free:
            more = min(limit - given[i], max(1, budget * loads[i] // mass), spare)
            given[i] = given[i] + more
            spare = spare - more
    return np.array([limit] + given)


def uneven(stream_key, amount, total, bound, slope):
    if amount == 2:
        one = jax.random.randint(stream_key, (), max(1, total - bound), min(bound, total - 1) + 1)
        return jnp.stack([one, total - one])
    tallies = jnp.asarray(profile(amount, total, bound, slope), jnp.int32)
    twos = (amount - 1) // 2
    source_of, receiver = tallies[1:1 + 2 * twos:2], tallies[2:2 + 2 * twos:2]
    room = jnp.minimum(source_of - 1, bound - receiver)
    passed = jax.random.randint(jax.random.fold_in(stream_key, 1), (twos,), 0, 1 << 20) % (room + 1)
    tallies = tallies.at[1:1 + 2 * twos:2].set(source_of - passed).at[2:2 + 2 * twos:2].set(receiver + passed)
    return tallies[jax.random.permutation(jax.random.fold_in(stream_key, 2), amount)]


def setup_inputs(seed: int = 0, part: int = 0) -> dict:
    splits = jax.random.split(jax.random.key(seed), 8)
    part_keys = jax.random.split(jax.random.fold_in(splits[7], part), 8)
    return {
        "queries": draw_queries(jax.random.fold_in(jax.random.fold_in(splits[7], part), 71), part),
        "suffix_kv": draw_suffix_kv(jax.random.fold_in(jax.random.fold_in(splits[7], part), 71), part),
        "page_store": draw_page_store(jax.random.fold_in(jax.random.fold_in(splits[7], part), 71), part),
        "holder_table": draw_holder_table(jax.random.fold_in(jax.random.fold_in(splits[7], part), 71), part),
        "prefix_pages": uneven(part_keys[4], REQS, PMAX * N_POOL * 5 // 8, PMAX, 2).astype(jnp.int32),
        "suffix_pages": uneven(part_keys[5], REQS, N_POOL * SPAGES * 3 // 4, SPAGES, 1).astype(jnp.int32),
        "fresh_alloc": draw_fresh_alloc(jax.random.fold_in(jax.random.fold_in(splits[7], part), 71), part),
    }


def attend_request(query_rows, key_rows, value_rows, visible, group_size):
    def one_head(head):
        keys_head = key_rows[head // group_size]
        values_head = value_rows[head // group_size]
        scores = jnp.dot(query_rows[head], keys_head.T, preferred_element_type=jnp.float32) * (HD ** -0.5)
        scores = jnp.where(visible, scores, -jnp.inf)
        row_max = jnp.max(scores, axis=1, keepdims=True)
        log_total = row_max[:, 0] + jnp.log(jnp.sum(jnp.exp(scores - row_max), axis=1))
        weights = jnp.exp(scores - log_total[:, None]).astype(jnp.bfloat16)
        result = jnp.dot(weights, values_head, preferred_element_type=jnp.float32)
        return result, log_total

    return lax.map(one_head, jnp.arange(QH))


def reference(queries, suffix_kv, page_store, holder_table, prefix_pages, suffix_pages, fresh_alloc):
    group_size = QH // KVH

    def one_request(request):
        page_table = holder_table[request]
        flat_index = page_table[:, 0] * SLOTS + page_table[:, 1]
        page_rows = jnp.take(page_store, flat_index, axis=0)
        page_rows = jnp.transpose(page_rows, (1, 2, 0, 3, 4)).reshape(2, KVH, PMAX * PAGE, HD)
        prefix_live = jnp.repeat(jnp.arange(PMAX) < prefix_pages[request], PAGE)
        suffix_rows = jnp.transpose(suffix_kv[request], (0, 2, 1, 3))
        key_rows = jnp.concatenate([page_rows[0], suffix_rows[0]], axis=1)
        value_rows = jnp.concatenate([page_rows[1], suffix_rows[1]], axis=1)
        row_ids = jnp.arange(SUF)
        causal = row_ids[None, :] <= row_ids[:, None]
        visible = jnp.concatenate([jnp.broadcast_to(prefix_live[None, :], (SUF, PMAX * PAGE)), causal], axis=1)
        query_rows = jnp.transpose(queries[request], (1, 0, 2))
        result, log_total = attend_request(query_rows, key_rows, value_rows, visible, group_size)
        live_rows = row_ids < suffix_pages[request] * PAGE
        result = jnp.where(live_rows[None, :, None], result, 0.0).astype(jnp.bfloat16)
        log_total = jnp.where(live_rows[None, :], log_total, 0.0)
        return jnp.transpose(result, (1, 0, 2)), log_total

    attention, row_lse = lax.map(one_request, jnp.arange(REQS))
    fresh_pages = suffix_kv.reshape(REQS, 2, SPAGES, PAGE, KVH, HD)
    fresh_pages = jnp.transpose(fresh_pages, (0, 2, 1, 4, 3, 5)).reshape(REQS * SPAGES, 2, KVH, PAGE, HD)
    page_live = (jnp.arange(SPAGES)[None, :] < suffix_pages[:, None]).reshape(-1)
    target = (fresh_alloc[:, :, 0] * FRESH + fresh_alloc[:, :, 1]).reshape(-1)
    target = jnp.where(page_live, target, N_POOL * FRESH)
    fresh_store = jnp.zeros((N_POOL * FRESH, 2, KVH, PAGE, HD), jnp.bfloat16).at[target].set(fresh_pages, mode="drop")
    return attention, row_lse, fresh_store
```

```python
import functools
import math

import jax
import jax.numpy as jnp
from jax import lax
from jax.experimental import pallas as pl
from jax.experimental.pallas import tpu as pltpu
from jax.sharding import PartitionSpec as P

MESH = pl.DeviceIdType.MESH
LOG2E = math.log2(math.e)
LN2 = math.log(2.0)


def kernel(
    sizes, tab, q_ref, sk_ref, store_ref, attn_ref, lse_ref, fresh_ref,
    pages, outbox, kv, sfx, freshbox, landed, qf, skf, qb, acc, top, total,
    load_sem, page_send, page_recv, pass_send, pass_recv,
    sfx_send, sfx_recv, fresh_send, fresh_recv,
):
    n, requests, cap, spages, level_count, heads, kv_all, kv_dev, page, hd = sizes
    rows = page
    group = heads // kv_all
    me = lax.axis_index("pool")
    seq = lax.axis_index("seq")
    other = 1 - seq
    base_prefix = requests * cap * 2
    base_suffix = base_prefix + requests
    base_alloc = base_suffix + requests
    far_right = me < n // 2

    def partner(k):
        high = n - 1 - k
        right = jnp.where(high > me, high, high - 1)
        left = jnp.where(k < me, k, k + 1)
        return jnp.where(far_right, right, left)

    load = pltpu.make_async_copy(store_ref, pages, load_sem)
    load.start()

    barrier = pltpu.get_barrier_semaphore()

    def greet(k, c):
        pl.semaphore_signal(barrier, inc=1, device_id={"pool": partner(k)}, device_id_type=MESH)
        return c

    lax.fori_loop(0, n - 1, greet, 0)
    pl.semaphore_signal(barrier, inc=1, device_id={"seq": other}, device_id_type=MESH)
    pl.semaphore_wait(barrier, n)
    load.wait()

    def slots_of(request):
        live = tab[base_prefix + request]

        def step(p, state):
            count, picks = state
            at = (request * cap + p) * 2
            mine = (tab[at] == me) & (p < live)
            slot = tab[at + 1]
            picks = tuple(
                jnp.where(mine & (count == level), slot, picks[level]) for level in range(level_count)
            )
            return count + mine.astype(jnp.int32), picks

        zero = jnp.int32(0)
        return lax.fori_loop(0, cap, step, (zero, (zero,) * level_count), unroll=cap <= 8)[1]

    def page_copy(k):
        to = partner(k)
        return pltpu.make_async_remote_copy(
            src_ref=outbox.at[to], dst_ref=kv.at[me, seq],
            send_sem=page_send.at[to], recv_sem=page_recv.at[me],
            device_id={"pool": to}, device_id_type=MESH,
        )

    def page_arrival(source):
        return pltpu.make_async_remote_copy(
            src_ref=outbox.at[source], dst_ref=kv.at[source, seq],
            send_sem=page_send.at[source], recv_sem=page_recv.at[source],
            device_id={"pool": source}, device_id_type=MESH,
        )

    def pass_copy(source, half):
        return pltpu.make_async_remote_copy(
            src_ref=kv.at[source, half], dst_ref=kv.at[source, half],
            send_sem=pass_send.at[source], recv_sem=pass_recv.at[source],
            device_id={"seq": other}, device_id_type=MESH,
        )

    def send_pages(k, c):
        to = partner(k)
        picks = slots_of(to)
        for level in range(level_count):
            outbox[to, :, :, level * page:(level + 1) * page, :] = pages[picks[level]]
        page_copy(k).start()
        return c

    lax.fori_loop(0, n - 1, send_pages, 0)

    picks = slots_of(me)
    for level in range(level_count):
        kv[me, seq, :, :, level * page:(level + 1) * page, :] = pages[picks[level]]
    pass_copy(me, seq).start()

    skf[...] = sk_ref[...].astype(jnp.float32)
    for a in range(2):
        for h in range(kv_all):
            picked = skf[pl.ds(a * rows * kv_all + h, rows, stride=kv_all), :]
            sfx[seq, a, h] = picked.astype(jnp.bfloat16)

    def sfx_copy(half):
        return pltpu.make_async_remote_copy(
            src_ref=sfx.at[half], dst_ref=sfx.at[half],
            send_sem=sfx_send, recv_sem=sfx_recv,
            device_id={"seq": other}, device_id_type=MESH,
        )

    sfx_copy(seq).start()
    sfx_copy(other).wait_recv()

    def fresh_pick(to):
        pick = jnp.int32(0)
        for q in range(1, spages):
            pick = jnp.where(tab[base_alloc + (me * spages + q) * 2] == to, q, pick)
        return sfx[pick, :, pl.ds(seq * kv_dev, kv_dev)]

    def fresh_copy(to, source, at):
        return pltpu.make_async_remote_copy(
            src_ref=freshbox.at[to], dst_ref=landed.at[source],
            send_sem=fresh_send.at[to], recv_sem=fresh_recv.at[source],
            device_id={"pool": at}, device_id_type=MESH,
        )

    def send_fresh(k, c):
        to = partner(k)
        freshbox[to] = fresh_pick(to)
        fresh_copy(to, me, to).start()
        return c

    lax.fori_loop(0, n - 1, send_fresh, 0)
    landed[me] = fresh_pick(me)

    qf[...] = q_ref[...].astype(jnp.float32)
    for h in range(heads):
        qb[h * rows:(h + 1) * rows, :] = qf[pl.ds(h, rows, stride=heads), :].astype(jnp.bfloat16)

    scale = (hd ** -0.5) * LOG2E

    def attend(j, keys, values, seen, first):
        at = slice(j * group * rows, (j + 1) * group * rows)
        scores = lax.dot_general(
            qb[at, :], keys, (((1,), (1,)), ((), ())), preferred_element_type=jnp.float32
        ) * scale
        scores = jnp.where(seen, scores, -jnp.inf)
        peak = jnp.max(scores, axis=1, keepdims=True)
        if not first:
            before = top[at, :]
            peak = jnp.maximum(before, peak)
        weights = jnp.exp2(scores - peak)
        mass = jnp.sum(weights, axis=1, keepdims=True)
        result = jnp.dot(weights.astype(jnp.bfloat16), values, preferred_element_type=jnp.float32)
        if first:
            total[at, :] = mass
            acc[at, :] = result
        else:
            fade = jnp.exp2(before - peak)
            total[at, :] = total[at, :] * fade + mass
            acc[at, :] = acc[at, :] * fade + result
        top[at, :] = peak

    block = (group * rows, spages * rows)
    token = lax.broadcasted_iota(jnp.int32, block, 0) % rows
    causal = lax.broadcasted_iota(jnp.int32, block, 1) <= token + seq * rows
    for j in range(kv_all):
        keys = sfx[:, 0, j].reshape(spages * rows, hd)
        values = sfx[:, 1, j].reshape(spages * rows, hd)
        attend(j, keys, values, causal, True)

    live_mine = tab[base_prefix + me]

    def attend_source(source):
        def step(p, count):
            hit = (tab[(me * cap + p) * 2] == source) & (p < live_mine)
            return count + hit.astype(jnp.int32)

        count = lax.fori_loop(0, cap, step, jnp.int32(0), unroll=cap <= 8)
        shape = (group * rows, level_count * page)
        seen = lax.broadcasted_iota(jnp.int32, shape, 1) < count * page
        for j in range(kv_all):
            attend(
                j, kv[source, j // kv_dev, 0, j % kv_dev], kv[source, j // kv_dev, 1, j % kv_dev],
                seen, False,
            )

    pass_copy(me, other).wait_recv()
    attend_source(me)

    def visit(k, c):
        source = partner(k)
        page_arrival(source).wait_recv()
        pass_copy(source, seq).start()
        pass_copy(source, other).wait_recv()
        attend_source(source)
        return c

    lax.fori_loop(0, n - 1, visit, 0)

    suffix_mine = tab[base_suffix + me]
    ids = lax.broadcasted_iota(jnp.int32, (rows, hd), 0)
    live = ids + seq * rows < suffix_mine * page
    eye = ids == lax.broadcasted_iota(jnp.int32, (rows, hd), 1)
    lane = lax.broadcasted_iota(jnp.int32, (1, rows), 1)
    for h in range(heads):
        at = slice(h * rows, (h + 1) * rows)
        mass = total[at, :]
        qf[pl.ds(h, rows, stride=heads), :] = jnp.where(live, acc[at, :] / mass, 0.0)
        lse = top[at, :] * LN2 + jnp.log(mass)
        line = jnp.sum(jnp.where(eye, lse, 0.0), axis=0, keepdims=True)
        lse_ref[h:h + 1, :] = jnp.where(lane + seq * rows < suffix_mine * page, line, 0.0)
    attn_ref[...] = qf[...].astype(jnp.bfloat16)

    def fresh_wait(k, c):
        source = partner(k)
        fresh_copy(source, source, source).wait_recv()
        return c

    lax.fori_loop(0, n - 1, fresh_wait, 0)
    for slot in range(spages):
        def find(r, state):
            source, filled = state
            hit = tab[base_alloc + (r * spages + slot) * 2] == me
            alive = hit & (slot < tab[base_suffix + r])
            return jnp.where(hit, r, source), jnp.where(alive, 1, filled)

        source, filled = lax.fori_loop(
            0, requests, find, (jnp.int32(0), jnp.int32(0)), unroll=requests <= 8
        )
        arrived = landed[source]
        fresh_ref[slot] = jnp.where(filled > 0, arrived, jnp.zeros_like(arrived))

    def drain(k, c):
        to = partner(k)
        page_copy(k).wait_send()
        fresh_copy(to, me, to).wait_send()
        pass_copy(to, seq).wait_send()
        return c

    lax.fori_loop(0, n - 1, drain, 0)
    pass_copy(me, seq).wait_send()
    sfx_copy(seq).wait_send()


def body(queries, suffix_kv, page_store, holder_table, prefix_pages, suffix_pages, fresh_alloc):
    n = lax.axis_size("pool")
    halves = lax.axis_size("seq")
    slots, _, kv_dev, page, hd = page_store.shape
    requests, cap = holder_table.shape[:2]
    spages = fresh_alloc.shape[1]
    levels = cap // n
    rows, heads = queries.shape[1:3]
    kv_all = suffix_kv.shape[3]
    assert requests == n and rows == page and spages == halves == 2
    assert kv_all == kv_dev * halves
    tab = jnp.concatenate(
        [holder_table.reshape(-1), prefix_pages, suffix_pages, fresh_alloc.reshape(-1)]
    )
    sizes = (n, requests, cap, spages, levels, heads, kv_all, kv_dev, page, hd)
    bf16, f32 = jnp.bfloat16, jnp.float32
    dma = pltpu.SemaphoreType.DMA
    vmem = pl.BlockSpec(memory_space=pltpu.VMEM)
    flops = 4 * heads * rows * hd * (cap * page + spages * rows)
    attention, row_lse, fresh = pl.pallas_call(
        functools.partial(kernel, sizes),
        out_shape=(
            jax.ShapeDtypeStruct((rows * heads, hd), bf16),
            jax.ShapeDtypeStruct((heads, rows), f32),
            jax.ShapeDtypeStruct((spages, 2, kv_dev, page, hd), bf16),
        ),
        in_specs=[
            pl.BlockSpec(memory_space=pltpu.SMEM), vmem, vmem, pl.BlockSpec(memory_space=pl.ANY),
        ],
        out_specs=(vmem, vmem, vmem),
        scratch_shapes=[
            pltpu.VMEM((slots, 2, kv_dev, page, hd), bf16),
            pltpu.VMEM((n, 2, kv_dev, levels * page, hd), bf16),
            pltpu.VMEM((n, halves, 2, kv_dev, levels * page, hd), bf16),
            pltpu.VMEM((halves, 2, kv_all, rows, hd), bf16),
            pltpu.VMEM((n, 2, kv_dev, page, hd), bf16),
            pltpu.VMEM((n, 2, kv_dev, page, hd), bf16),
            pltpu.VMEM((rows * heads, hd), f32),
            pltpu.VMEM((2 * rows * kv_all, hd), f32),
            pltpu.VMEM((rows * heads, hd), bf16),
            pltpu.VMEM((rows * heads, hd), f32),
            pltpu.VMEM((rows * heads, 1), f32),
            pltpu.VMEM((rows * heads, 1), f32),
            dma, dma((n,)), dma((n,)), dma((n,)), dma((n,)),
            dma, dma, dma((n,)), dma((n,)),
        ],
        compiler_params=pltpu.CompilerParams(
            collective_id=0, has_side_effects=True, vmem_limit_bytes=58 * 1024 * 1024
        ),
        cost_estimate=pl.CostEstimate(
            flops=flops, bytes_accessed=6 * 1024 * 1024, transcendentals=flops // (4 * hd)
        ),
        name="suffix_attention",
    )(tab, queries.reshape(rows * heads, hd), suffix_kv.reshape(2 * rows * kv_all, hd), page_store)
    return (
        attention.reshape(1, rows, heads, hd), row_lse[None], fresh,
    )


def solution(mesh):
    placed = (
        P(("replica", "pool"), "seq", "tensor", None),
        P(("replica", "pool"), None, "seq", "tensor", None),
        P(("replica", "pool"), None, ("tensor", "seq"), None, None),
        P("replica", None, None),
        P("replica"),
        P("replica"),
        P("replica", None, None),
    )
    return jax.shard_map(
        body,
        mesh=mesh,
        in_specs=placed,
        out_specs=(
            P(("replica", "pool"), "seq", "tensor", None),
            P(("replica", "pool"), "tensor", "seq"),
            P(("replica", "pool"), None, ("tensor", "seq"), None, None),
        ),
        check_vma=False,
    )
```

```python
import functools
import math

import jax
import jax.numpy as jnp
from jax import lax
from jax.experimental import pallas as pl
from jax.experimental.pallas import tpu as pltpu
from jax.sharding import PartitionSpec as P

MESH = pl.DeviceIdType.MESH
LOG2E = math.log2(math.e)
LN2 = math.log(2.0)


def kernel(
    sizes, table, prefix, suffix, alloc, q_hbm, sk_hbm, store_ref,
    attn_ref, lse_ref, landed,
    pages, outbox, kv, sfx, freshbox, qin, skin, attn, lse_rows, qf, skf, qb, acc, top, total,
    load_sem, q_sem, sk_sem, attn_sem, lse_sem, own_sem, page_send, page_recv, pass_send, pass_recv,
    sfx_send, sfx_recv, fresh_send, fresh_recv,
):
    n, requests, cap, spages, level_count, heads, kv_all, kv_dev, page, hd = sizes
    rows = page
    group = heads // kv_all
    me = lax.axis_index("pool")
    seq = lax.axis_index("seq")
    other = 1 - seq
    far_right = me < n // 2

    def partner(k):
        high = n - 1 - k
        right = jnp.where(high > me, high, high - 1)
        left = jnp.where(k < me, k, k + 1)
        return jnp.where(far_right, right, left)

    load = pltpu.make_async_copy(store_ref, pages, load_sem)
    load.start()
    q_load = pltpu.make_async_copy(q_hbm, qin, q_sem)
    sk_load = pltpu.make_async_copy(sk_hbm, skin, sk_sem)
    sk_load.start()
    q_load.start()

    barrier = pltpu.get_barrier_semaphore()

    def greet(k, c):
        pl.semaphore_signal(barrier, inc=1, device_id={"pool": partner(k)}, device_id_type=MESH)
        return c

    lax.fori_loop(0, n - 1, greet, 0)
    pl.semaphore_signal(barrier, inc=1, device_id={"seq": other}, device_id_type=MESH)
    pl.semaphore_wait(barrier, n)
    load.wait()

    def slots_of(request):
        live = prefix[request]

        def step(p, state):
            count, picks = state
            mine = (table[request, 0, p] == me) & (p < live)
            slot = table[request, 1, p]
            picks = tuple(
                jnp.where(mine & (count == level), slot, picks[level]) for level in range(level_count)
            )
            return count + mine.astype(jnp.int32), picks

        zero = jnp.int32(0)
        return lax.fori_loop(0, cap, step, (zero, (zero,) * level_count), unroll=cap <= 8)[1]

    def page_copy(k):
        to = partner(k)
        return pltpu.make_async_remote_copy(
            src_ref=outbox.at[to], dst_ref=kv.at[me, seq],
            send_sem=page_send.at[to], recv_sem=page_recv.at[me],
            device_id={"pool": to}, device_id_type=MESH,
        )

    def page_arrival(source):
        return pltpu.make_async_remote_copy(
            src_ref=outbox.at[source], dst_ref=kv.at[source, seq],
            send_sem=page_send.at[source], recv_sem=page_recv.at[source],
            device_id={"pool": source}, device_id_type=MESH,
        )

    def pass_copy(source, half):
        return pltpu.make_async_remote_copy(
            src_ref=kv.at[source, half], dst_ref=kv.at[source, half],
            send_sem=pass_send.at[source], recv_sem=pass_recv.at[source],
            device_id={"seq": other}, device_id_type=MESH,
        )

    def send_pages(k, c):
        to = partner(k)
        picks = slots_of(to)
        for level in range(level_count):
            outbox[to, :, :, level * page:(level + 1) * page, :] = pages[picks[level]]
        page_copy(k).start()
        return c

    lax.fori_loop(0, n - 1, send_pages, 0)

    picks = slots_of(me)
    for level in range(level_count):
        kv[me, seq, :, :, level * page:(level + 1) * page, :] = pages[picks[level]]
    pass_copy(me, seq).start()

    sk_load.wait()
    skf[...] = skin[...].astype(jnp.float32)
    for a in range(2):
        for h in range(kv_all):
            picked = skf[pl.ds(a * rows * kv_all + h, rows, stride=kv_all), :]
            sfx[seq, a, h] = picked.astype(jnp.bfloat16)

    def sfx_copy(half):
        return pltpu.make_async_remote_copy(
            src_ref=sfx.at[half], dst_ref=sfx.at[half],
            send_sem=sfx_send, recv_sem=sfx_recv,
            device_id={"seq": other}, device_id_type=MESH,
        )

    sfx_copy(seq).start()
    sfx_copy(other).wait_recv()

    def fresh_pick(to):
        pick = jnp.int32(0)
        for q in range(1, spages):
            pick = jnp.where(alloc[q, 0, me] == to, q, pick)
        return sfx[pick, :, pl.ds(seq * kv_dev, kv_dev)]

    def fresh_copy(to, source, at):
        return pltpu.make_async_remote_copy(
            src_ref=freshbox.at[to], dst_ref=landed.at[source],
            send_sem=fresh_send.at[to], recv_sem=fresh_recv.at[source],
            device_id={"pool": at}, device_id_type=MESH,
        )

    def send_fresh(k, c):
        to = partner(k)
        freshbox[to] = fresh_pick(to)
        fresh_copy(to, me, to).start()
        return c

    lax.fori_loop(0, n - 1, send_fresh, 0)
    freshbox[me] = fresh_pick(me)
    own_fresh = pltpu.make_async_copy(freshbox.at[me], landed.at[me], own_sem)
    own_fresh.start()

    q_load.wait()
    qf[...] = qin[...].astype(jnp.float32)
    for h in range(heads):
        qb[h * rows:(h + 1) * rows, :] = qf[pl.ds(h, rows, stride=heads), :].astype(jnp.bfloat16)

    scale = (hd ** -0.5) * LOG2E

    def attend(j, score_parts, values, biases, first):
        peaks = [jnp.max(part, axis=0, keepdims=True) for part in score_parts]
        peaks = [peak if bias is None else peak + bias for peak, bias in zip(peaks, biases)]
        peak = functools.reduce(jnp.maximum, peaks)
        if not first:
            before = top[j]
            peak = jnp.maximum(before, peak)
        weights = jnp.concatenate([
            jnp.exp2(part - (peak if bias is None else peak - bias))
            for part, bias in zip(score_parts, biases)
        ], axis=0)
        mass = jnp.sum(weights, axis=0, keepdims=True)
        result = lax.dot_general(
            values, weights.astype(jnp.bfloat16), (((0,), (0,)), ((), ())),
            preferred_element_type=jnp.float32,
        )
        if first:
            total[j] = mass
            acc[j] = result
        else:
            fade = jnp.exp2(before - peak)
            total[j] = total[j] * fade + mass
            acc[j] = acc[j] * fade + result
        top[j] = peak

    def score(j, keys):
        return lax.dot_general(
            keys, qb[j * group * rows:(j + 1) * group * rows, :], (((1,), (1,)), ((), ())),
            preferred_element_type=jnp.float32,
        ) * scale

    block = (spages * rows, group * rows)
    token = lax.broadcasted_iota(jnp.int32, block, 1) % rows
    causal = lax.broadcasted_iota(jnp.int32, block, 0) <= token + seq * rows
    for j in range(kv_all):
        keys = sfx[:, 0, j].reshape(spages * rows, hd)
        values = sfx[:, 1, j].reshape(spages * rows, hd)
        attend(j, [jnp.where(causal, score(j, keys), -jnp.inf)], values, [None], True)

    live_mine = prefix[me]

    def attend_source(source):
        def step(p, count):
            hit = (table[me, 0, p] == source) & (p < live_mine)
            return count + hit.astype(jnp.int32)

        count = lax.fori_loop(0, cap, step, jnp.int32(0), unroll=cap <= 8)
        biases = [
            jnp.where(count > level, jnp.float32(0.0), jnp.float32(-jnp.inf))
            for level in range(level_count)
        ]
        for j in range(kv_all):
            scores = score(j, kv[source, j // kv_dev, 0, j % kv_dev])
            parts = [scores[level * page:(level + 1) * page] for level in range(level_count)]
            attend(j, parts, kv[source, j // kv_dev, 1, j % kv_dev], biases, False)

    pass_copy(me, other).wait_recv()
    attend_source(me)

    def visit(k, c):
        source = partner(k)
        page_arrival(source).wait_recv()
        pass_copy(source, seq).start()
        pass_copy(source, other).wait_recv()
        attend_source(source)
        return c

    lax.fori_loop(0, n - 1, visit, 0)

    suffix_mine = suffix[me]
    ids = lax.broadcasted_iota(jnp.int32, (rows, hd), 0)
    live = ids + seq * rows < suffix_mine * page
    lane = lax.broadcasted_iota(jnp.int32, (1, rows), 1)
    for j in range(kv_all):
        mass = total[j]
        lse = top[j] * LN2 + jnp.log(mass)
        result = acc[j] / mass
        for g in range(group):
            h = j * group + g
            at = slice(g * rows, (g + 1) * rows)
            qf[pl.ds(h, rows, stride=heads), :] = jnp.where(live, result[:, at].T, 0.0)
            lse_rows[h:h + 1, :] = jnp.where(lane + seq * rows < suffix_mine * page, lse[:, at], 0.0)
    attn[...] = qf[...].astype(jnp.bfloat16)
    attn_out = pltpu.make_async_copy(attn, attn_ref, attn_sem)
    lse_out = pltpu.make_async_copy(lse_rows, lse_ref, lse_sem)
    attn_out.start()
    lse_out.start()

    def fresh_wait(k, c):
        source = partner(k)
        fresh_copy(source, source, source).wait_recv()
        return c

    lax.fori_loop(0, n - 1, fresh_wait, 0)
    def drain(k, c):
        to = partner(k)
        page_copy(k).wait_send()
        fresh_copy(to, me, to).wait_send()
        pass_copy(to, seq).wait_send()
        return c

    lax.fori_loop(0, n - 1, drain, 0)
    pass_copy(me, seq).wait_send()
    sfx_copy(seq).wait_send()
    own_fresh.wait()
    attn_out.wait()
    lse_out.wait()


def place(spages, requests, alloc, suffix, attn_in, lse_in, landed, attn_ref, lse_ref, fresh_ref,
          attn, lse, fresh, in_sem, out_sem, fresh_in, fresh_out):
    me = lax.axis_index("pool")
    parts = attn.shape[0]
    attn_loads = [
        pltpu.make_async_copy(attn_in.at[i], attn.at[i], in_sem.at[i]) for i in range(parts)
    ]
    attn_stores = [
        pltpu.make_async_copy(attn.at[i], attn_ref.at[i], out_sem.at[i]) for i in range(parts)
    ]
    lse_load = pltpu.make_async_copy(lse_in, lse, in_sem.at[parts])
    lse_store = pltpu.make_async_copy(lse, lse_ref, out_sem.at[parts])
    for load in attn_loads:
        load.start()
    lse_load.start()
    found = []
    for slot in range(spages):
        def find(r, state):
            source, filled = state
            hit = alloc[slot, 0, r] == me
            alive = hit & (slot < suffix[r])
            return jnp.where(hit, r, source), jnp.where(alive, 1, filled)

        found.append(lax.fori_loop(
            0, requests, find, (jnp.int32(0), jnp.int32(0)), unroll=requests <= 8
        ))
    fresh_loads = [
        pltpu.make_async_copy(landed.at[found[i][0]], fresh.at[i], fresh_in.at[i])
        for i in range(spages)
    ]
    fresh_stores = [
        pltpu.make_async_copy(fresh.at[i], fresh_ref.at[i], fresh_out.at[i])
        for i in range(spages)
    ]
    for load in fresh_loads:
        load.start()
    for load, store in zip(attn_loads, attn_stores):
        load.wait()
        store.start()
    lse_load.wait()
    lse_store.start()
    for slot in range(spages):
        fresh_loads[slot].wait()

        @pl.when(found[slot][1] == 0)
        def _():
            fresh[slot] = jnp.zeros_like(fresh[slot])

        fresh_stores[slot].start()
    for store in attn_stores + [lse_store] + fresh_stores:
        store.wait()


def body(queries, suffix_kv, page_store, holder_table, prefix_pages, suffix_pages, fresh_alloc):
    n = lax.axis_size("pool")
    halves = lax.axis_size("seq")
    slots, _, kv_dev, page, hd = page_store.shape
    requests, cap = holder_table.shape[:2]
    spages = fresh_alloc.shape[1]
    levels = cap // n
    rows, heads = queries.shape[1:3]
    kv_all = suffix_kv.shape[3]
    assert requests == n and rows == page and spages == halves == 2
    assert kv_all == kv_dev * halves
    table = jnp.transpose(holder_table, (0, 2, 1))
    alloc = jnp.transpose(fresh_alloc, (1, 2, 0))
    sizes = (n, requests, cap, spages, levels, heads, kv_all, kv_dev, page, hd)
    bf16, f32 = jnp.bfloat16, jnp.float32
    dma = pltpu.SemaphoreType.DMA
    smem = pl.BlockSpec(memory_space=pltpu.SMEM)
    away = pl.BlockSpec(memory_space=pl.ANY)
    flops = 4 * heads * rows * hd * (cap * page + spages * rows)
    attention, row_lse, landed = pl.pallas_call(
        functools.partial(kernel, sizes),
        out_shape=(
            jax.ShapeDtypeStruct((rows * heads, hd), bf16),
            jax.ShapeDtypeStruct((heads, rows), f32),
            jax.ShapeDtypeStruct((n, 2, kv_dev, page, hd), bf16),
        ),
        in_specs=[smem, smem, smem, smem, away, away, away],
        out_specs=(away, away, away),
        scratch_shapes=[
            pltpu.VMEM((slots, 2, kv_dev, page, hd), bf16),
            pltpu.VMEM((n, 2, kv_dev, levels * page, hd), bf16),
            pltpu.VMEM((n, halves, 2, kv_dev, levels * page, hd), bf16),
            pltpu.VMEM((halves, 2, kv_all, rows, hd), bf16),
            pltpu.VMEM((n, 2, kv_dev, page, hd), bf16),
            pltpu.VMEM((rows * heads, hd), bf16),
            pltpu.VMEM((2 * rows * kv_all, hd), bf16),
            pltpu.VMEM((rows * heads, hd), bf16),
            pltpu.VMEM((heads, rows), f32),
            pltpu.VMEM((rows * heads, hd), f32),
            pltpu.VMEM((2 * rows * kv_all, hd), f32),
            pltpu.VMEM((rows * heads, hd), bf16),
            pltpu.VMEM((kv_all, hd, heads // kv_all * rows), f32),
            pltpu.VMEM((kv_all, 1, heads // kv_all * rows), f32),
            pltpu.VMEM((kv_all, 1, heads // kv_all * rows), f32),
            dma, dma, dma, dma, dma, dma, dma((n,)), dma((n,)), dma((n,)), dma((n,)),
            dma, dma, dma((n,)), dma((n,)),
        ],
        compiler_params=pltpu.CompilerParams(
            collective_id=0, has_side_effects=True, vmem_limit_bytes=58 * 1024 * 1024
        ),
        cost_estimate=pl.CostEstimate(
            flops=flops, bytes_accessed=6 * 1024 * 1024, transcendentals=flops // (4 * hd)
        ),
        name="suffix_attention",
    )(
        table, prefix_pages, suffix_pages, alloc,
        queries.reshape(rows * heads, hd), suffix_kv.reshape(2 * rows * kv_all, hd), page_store,
    )
    parts = 4
    attention, row_lse, fresh = pl.pallas_call(
        functools.partial(place, spages, requests),
        out_shape=(
            jax.ShapeDtypeStruct((parts, rows * heads // parts, hd), bf16),
            jax.ShapeDtypeStruct((heads, rows), f32),
            jax.ShapeDtypeStruct((spages, 2, kv_dev, page, hd), bf16),
        ),
        in_specs=[smem, smem, away, away, away],
        out_specs=(away, away, away),
        scratch_shapes=[
            pltpu.VMEM((parts, rows * heads // parts, hd), bf16),
            pltpu.VMEM((heads, rows), f32),
            pltpu.VMEM((spages, 2, kv_dev, page, hd), bf16),
            dma((parts + 1,)), dma((parts + 1,)), dma((spages,)), dma((spages,)),
        ],
        compiler_params=pltpu.CompilerParams(has_side_effects=True),
        name="place_outputs",
    )(
        alloc, suffix_pages, attention.reshape(parts, rows * heads // parts, hd), row_lse, landed
    )
    return (
        attention.reshape(1, rows, heads, hd), row_lse[None], fresh,
    )


def solution(mesh):
    placed = (
        P(("replica", "pool"), "seq", "tensor", None),
        P(("replica", "pool"), None, "seq", "tensor", None),
        P(("replica", "pool"), None, ("tensor", "seq"), None, None),
        P("replica", None, None),
        P("replica"),
        P("replica"),
        P("replica", None, None),
    )
    return jax.shard_map(
        body,
        mesh=mesh,
        in_specs=placed,
        out_specs=(
            P(("replica", "pool"), "seq", "tensor", None),
            P(("replica", "pool"), "tensor", "seq"),
            P(("replica", "pool"), None, ("tensor", "seq"), None, None),
        ),
        check_vma=False,
    )
```

```python
import functools
import math

import jax
import jax.numpy as jnp
from jax import lax
from jax.experimental import pallas as pl
from jax.experimental.pallas import tpu as pltpu
from jax.sharding import PartitionSpec as P

MESH = pl.DeviceIdType.MESH
LOG2E = math.log2(math.e)
LN2 = math.log(2.0)


def kernel(
    sizes, table, prefix, suffix, alloc, q_hbm, sk_hbm, store_ref,
    attn_ref, lse_ref, landed,
    pages, outbox, kv, sfx, freshbox, qin, skin, attn, lse_rows, qf, skf, qb, acc, top, total,
    load_sem, q_sem, sk_sem, attn_sem, lse_sem, own_sem, page_send, page_recv, pass_send, pass_recv,
    sfx_send, sfx_recv, fresh_send, fresh_recv,
):
    n, requests, cap, spages, level_count, heads, kv_all, kv_dev, page, hd = sizes
    rows = page
    group = heads // kv_all
    me = lax.axis_index("pool")
    seq = lax.axis_index("seq")
    other = 1 - seq
    far_right = me < n // 2

    def partner(k):
        high = n - 1 - k
        right = jnp.where(high > me, high, high - 1)
        left = jnp.where(k < me, k, k + 1)
        return jnp.where(far_right, right, left)

    load = pltpu.make_async_copy(store_ref, pages, load_sem)
    load.start()
    q_load = pltpu.make_async_copy(q_hbm, qin, q_sem)
    sk_load = pltpu.make_async_copy(sk_hbm, skin, sk_sem)
    sk_load.start()
    q_load.start()

    barrier = pltpu.get_barrier_semaphore()

    def greet(k, c):
        pl.semaphore_signal(barrier, inc=1, device_id={"pool": partner(k)}, device_id_type=MESH)
        return c

    lax.fori_loop(0, n - 1, greet, 0)
    pl.semaphore_signal(barrier, inc=1, device_id={"seq": other}, device_id_type=MESH)
    pl.semaphore_wait(barrier, n)
    load.wait()

    def slots_of(request):
        live = prefix[request]

        def step(p, state):
            count, picks = state
            mine = (table[request, 0, p] == me) & (p < live)
            slot = table[request, 1, p]
            picks = tuple(
                jnp.where(mine & (count == level), slot, picks[level]) for level in range(level_count)
            )
            return count + mine.astype(jnp.int32), picks

        zero = jnp.int32(0)
        return lax.fori_loop(0, cap, step, (zero, (zero,) * level_count), unroll=cap <= 8)[1]

    def page_copy(k):
        to = partner(k)
        return pltpu.make_async_remote_copy(
            src_ref=outbox.at[to], dst_ref=kv.at[me, seq],
            send_sem=page_send.at[to], recv_sem=page_recv.at[me],
            device_id={"pool": to}, device_id_type=MESH,
        )

    def page_arrival(source):
        return pltpu.make_async_remote_copy(
            src_ref=outbox.at[source], dst_ref=kv.at[source, seq],
            send_sem=page_send.at[source], recv_sem=page_recv.at[source],
            device_id={"pool": source}, device_id_type=MESH,
        )

    def pass_copy(source, half):
        return pltpu.make_async_remote_copy(
            src_ref=kv.at[source, half], dst_ref=kv.at[source, half],
            send_sem=pass_send.at[source], recv_sem=pass_recv.at[source],
            device_id={"seq": other}, device_id_type=MESH,
        )

    def send_pages(k, c):
        to = partner(k)
        picks = slots_of(to)
        for level in range(level_count):
            outbox[to, :, :, level * page:(level + 1) * page, :] = pages[picks[level]]
        page_copy(k).start()
        return c

    lax.fori_loop(0, n - 1, send_pages, 0)

    picks = slots_of(me)
    for level in range(level_count):
        kv[me, seq, :, :, level * page:(level + 1) * page, :] = pages[picks[level]]
    pass_copy(me, seq).start()

    sk_load.wait()
    skf[...] = skin[...].astype(jnp.float32)
    for a in range(2):
        for h in range(kv_all):
            picked = skf[pl.ds(a * rows * kv_all + h, rows, stride=kv_all), :]
            sfx[seq, a, h] = picked.astype(jnp.bfloat16)

    def sfx_copy(half):
        return pltpu.make_async_remote_copy(
            src_ref=sfx.at[half], dst_ref=sfx.at[half],
            send_sem=sfx_send, recv_sem=sfx_recv,
            device_id={"seq": other}, device_id_type=MESH,
        )

    sfx_copy(seq).start()
    sfx_copy(other).wait_recv()

    def fresh_pick(to):
        pick = jnp.int32(0)
        for q in range(1, spages):
            pick = jnp.where(alloc[q, 0, me] == to, q, pick)
        return sfx[pick, :, pl.ds(seq * kv_dev, kv_dev)]

    def fresh_copy(to, source, at):
        return pltpu.make_async_remote_copy(
            src_ref=freshbox.at[to], dst_ref=landed.at[source],
            send_sem=fresh_send.at[to], recv_sem=fresh_recv.at[source],
            device_id={"pool": at}, device_id_type=MESH,
        )

    def send_fresh(k, c):
        to = partner(k)
        freshbox[to] = fresh_pick(to)
        fresh_copy(to, me, to).start()
        return c

    lax.fori_loop(0, n - 1, send_fresh, 0)
    freshbox[me] = fresh_pick(me)
    own_fresh = pltpu.make_async_copy(freshbox.at[me], landed.at[me], own_sem)
    own_fresh.start()

    q_load.wait()
    qf[...] = qin[...].astype(jnp.float32)
    for h in range(heads):
        qb[h * rows:(h + 1) * rows, :] = qf[pl.ds(h, rows, stride=heads), :].astype(jnp.bfloat16)

    scale = (hd ** -0.5) * LOG2E

    def attend(j, score_parts, values, biases, first):
        peaks = [jnp.max(part, axis=0, keepdims=True) for part in score_parts]
        peaks = [peak if bias is None else peak + bias for peak, bias in zip(peaks, biases)]
        peak = functools.reduce(jnp.maximum, peaks)
        if not first:
            before = top[j]
            peak = jnp.maximum(before, peak)
        weights = jnp.concatenate([
            jnp.exp2(part - (peak if bias is None else peak - bias))
            for part, bias in zip(score_parts, biases)
        ], axis=0)
        mass = jnp.sum(weights, axis=0, keepdims=True)
        result = lax.dot_general(
            values, weights.astype(jnp.bfloat16), (((0,), (0,)), ((), ())),
            preferred_element_type=jnp.float32,
        )
        if first:
            total[j] = mass
            acc[j] = result
        else:
            fade = jnp.exp2(before - peak)
            total[j] = total[j] * fade + mass
            acc[j] = acc[j] * fade + result
        top[j] = peak

    def score(j, keys):
        return lax.dot_general(
            keys, qb[j * group * rows:(j + 1) * group * rows, :], (((1,), (1,)), ((), ())),
            preferred_element_type=jnp.float32,
        ) * scale

    block = (spages * rows, group * rows)
    token = lax.broadcasted_iota(jnp.int32, block, 1) % rows
    causal = lax.broadcasted_iota(jnp.int32, block, 0) <= token + seq * rows
    for j in range(kv_all):
        keys = sfx[:, 0, j].reshape(spages * rows, hd)
        values = sfx[:, 1, j].reshape(spages * rows, hd)
        attend(j, [jnp.where(causal, score(j, keys), -jnp.inf)], values, [None], True)

    live_mine = prefix[me]

    def attend_source(source):
        def step(p, count):
            hit = (table[me, 0, p] == source) & (p < live_mine)
            return count + hit.astype(jnp.int32)

        count = lax.fori_loop(0, cap, step, jnp.int32(0), unroll=cap <= 8)
        biases = [
            jnp.where(count > level, jnp.float32(0.0), jnp.float32(-jnp.inf))
            for level in range(level_count)
        ]
        for j in range(kv_all):
            scores = score(j, kv[source, j // kv_dev, 0, j % kv_dev])
            parts = [scores[level * page:(level + 1) * page] for level in range(level_count)]
            attend(j, parts, kv[source, j // kv_dev, 1, j % kv_dev], biases, False)

    def relay(k):
        source = partner(k)
        page_arrival(source).wait_recv()
        pass_copy(source, seq).start()

    pass_copy(me, other).wait_recv()
    attend_source(me)
    relay(0)

    def visit(k, c):
        source = partner(k)
        pass_copy(source, other).wait_recv()
        relay(k + 1)
        attend_source(source)
        return c

    lax.fori_loop(0, n - 2, visit, 0)
    pass_copy(partner(n - 2), other).wait_recv()
    attend_source(partner(n - 2))

    suffix_mine = suffix[me]
    ids = lax.broadcasted_iota(jnp.int32, (rows, hd), 0)
    live = ids + seq * rows < suffix_mine * page
    lane = lax.broadcasted_iota(jnp.int32, (1, rows), 1)
    for j in range(kv_all):
        mass = total[j]
        lse = top[j] * LN2 + jnp.log(mass)
        result = acc[j] / mass
        for g in range(group):
            h = j * group + g
            at = slice(g * rows, (g + 1) * rows)
            qf[pl.ds(h, rows, stride=heads), :] = jnp.where(live, result[:, at].T, 0.0)
            lse_rows[h:h + 1, :] = jnp.where(lane + seq * rows < suffix_mine * page, lse[:, at], 0.0)
    attn[...] = qf[...].astype(jnp.bfloat16)
    attn_out = pltpu.make_async_copy(attn, attn_ref, attn_sem)
    lse_out = pltpu.make_async_copy(lse_rows, lse_ref, lse_sem)
    attn_out.start()
    lse_out.start()

    def fresh_wait(k, c):
        source = partner(k)
        fresh_copy(source, source, source).wait_recv()
        return c

    lax.fori_loop(0, n - 1, fresh_wait, 0)
    def drain(k, c):
        to = partner(k)
        page_copy(k).wait_send()
        fresh_copy(to, me, to).wait_send()
        pass_copy(to, seq).wait_send()
        return c

    lax.fori_loop(0, n - 1, drain, 0)
    pass_copy(me, seq).wait_send()
    sfx_copy(seq).wait_send()
    own_fresh.wait()
    attn_out.wait()
    lse_out.wait()


def place(spages, requests, alloc, suffix, attn_in, lse_in, landed, attn_ref, lse_ref, fresh_ref,
          attn, lse, fresh, in_sem, out_sem, fresh_in, fresh_out):
    me = lax.axis_index("pool")
    parts = attn.shape[0]
    attn_loads = [
        pltpu.make_async_copy(attn_in.at[i], attn.at[i], in_sem.at[i]) for i in range(parts)
    ]
    attn_stores = [
        pltpu.make_async_copy(attn.at[i], attn_ref.at[i], out_sem.at[i]) for i in range(parts)
    ]
    lse_load = pltpu.make_async_copy(lse_in, lse, in_sem.at[parts])
    lse_store = pltpu.make_async_copy(lse, lse_ref, out_sem.at[parts])
    for load in attn_loads:
        load.start()
    lse_load.start()
    found = []
    for slot in range(spages):
        def find(r, state):
            source, filled = state
            hit = alloc[slot, 0, r] == me
            alive = hit & (slot < suffix[r])
            return jnp.where(hit, r, source), jnp.where(alive, 1, filled)

        found.append(lax.fori_loop(
            0, requests, find, (jnp.int32(0), jnp.int32(0)), unroll=requests <= 8
        ))
    fresh_loads = [
        pltpu.make_async_copy(landed.at[found[i][0]], fresh.at[i], fresh_in.at[i])
        for i in range(spages)
    ]
    fresh_stores = [
        pltpu.make_async_copy(fresh.at[i], fresh_ref.at[i], fresh_out.at[i])
        for i in range(spages)
    ]
    for load in fresh_loads:
        load.start()
    for load, store in zip(attn_loads, attn_stores):
        load.wait()
        store.start()
    lse_load.wait()
    lse_store.start()
    for slot in range(spages):
        fresh_loads[slot].wait()

        @pl.when(found[slot][1] == 0)
        def _():
            fresh[slot] = jnp.zeros_like(fresh[slot])

        fresh_stores[slot].start()
    for store in attn_stores + [lse_store] + fresh_stores:
        store.wait()


def body(queries, suffix_kv, page_store, holder_table, prefix_pages, suffix_pages, fresh_alloc):
    n = lax.axis_size("pool")
    halves = lax.axis_size("seq")
    slots, _, kv_dev, page, hd = page_store.shape
    requests, cap = holder_table.shape[:2]
    spages = fresh_alloc.shape[1]
    levels = cap // n
    rows, heads = queries.shape[1:3]
    kv_all = suffix_kv.shape[3]
    assert requests == n and rows == page and spages == halves == 2
    assert kv_all == kv_dev * halves
    table = jnp.transpose(holder_table, (0, 2, 1))
    alloc = jnp.transpose(fresh_alloc, (1, 2, 0))
    sizes = (n, requests, cap, spages, levels, heads, kv_all, kv_dev, page, hd)
    bf16, f32 = jnp.bfloat16, jnp.float32
    dma = pltpu.SemaphoreType.DMA
    smem = pl.BlockSpec(memory_space=pltpu.SMEM)
    away = pl.BlockSpec(memory_space=pl.ANY)
    flops = 4 * heads * rows * hd * (cap * page + spages * rows)
    attention, row_lse, landed = pl.pallas_call(
        functools.partial(kernel, sizes),
        out_shape=(
            jax.ShapeDtypeStruct((rows * heads, hd), bf16),
            jax.ShapeDtypeStruct((heads, rows), f32),
            jax.ShapeDtypeStruct((n, 2, kv_dev, page, hd), bf16),
        ),
        in_specs=[smem, smem, smem, smem, away, away, away],
        out_specs=(away, away, away),
        scratch_shapes=[
            pltpu.VMEM((slots, 2, kv_dev, page, hd), bf16),
            pltpu.VMEM((n, 2, kv_dev, levels * page, hd), bf16),
            pltpu.VMEM((n, halves, 2, kv_dev, levels * page, hd), bf16),
            pltpu.VMEM((halves, 2, kv_all, rows, hd), bf16),
            pltpu.VMEM((n, 2, kv_dev, page, hd), bf16),
            pltpu.VMEM((rows * heads, hd), bf16),
            pltpu.VMEM((2 * rows * kv_all, hd), bf16),
            pltpu.VMEM((rows * heads, hd), bf16),
            pltpu.VMEM((heads, rows), f32),
            pltpu.VMEM((rows * heads, hd), f32),
            pltpu.VMEM((2 * rows * kv_all, hd), f32),
            pltpu.VMEM((rows * heads, hd), bf16),
            pltpu.VMEM((kv_all, hd, heads // kv_all * rows), f32),
            pltpu.VMEM((kv_all, 1, heads // kv_all * rows), f32),
            pltpu.VMEM((kv_all, 1, heads // kv_all * rows), f32),
            dma, dma, dma, dma, dma, dma, dma((n,)), dma((n,)), dma((n,)), dma((n,)),
            dma, dma, dma((n,)), dma((n,)),
        ],
        compiler_params=pltpu.CompilerParams(
            collective_id=0, has_side_effects=True, vmem_limit_bytes=58 * 1024 * 1024
        ),
        cost_estimate=pl.CostEstimate(
            flops=flops, bytes_accessed=6 * 1024 * 1024, transcendentals=flops // (4 * hd)
        ),
        name="suffix_attention",
    )(
        table, prefix_pages, suffix_pages, alloc,
        queries.reshape(rows * heads, hd), suffix_kv.reshape(2 * rows * kv_all, hd), page_store,
    )
    parts = 4
    attention, row_lse, fresh = pl.pallas_call(
        functools.partial(place, spages, requests),
        out_shape=(
            jax.ShapeDtypeStruct((parts, rows * heads // parts, hd), bf16),
            jax.ShapeDtypeStruct((heads, rows), f32),
            jax.ShapeDtypeStruct((spages, 2, kv_dev, page, hd), bf16),
        ),
        in_specs=[smem, smem, away, away, away],
        out_specs=(away, away, away),
        scratch_shapes=[
            pltpu.VMEM((parts, rows * heads // parts, hd), bf16),
            pltpu.VMEM((heads, rows), f32),
            pltpu.VMEM((spages, 2, kv_dev, page, hd), bf16),
            dma((parts + 1,)), dma((parts + 1,)), dma((spages,)), dma((spages,)),
        ],
        compiler_params=pltpu.CompilerParams(has_side_effects=True),
        name="place_outputs",
    )(
        alloc, suffix_pages, attention.reshape(parts, rows * heads // parts, hd), row_lse, landed
    )
    return (
        attention.reshape(1, rows, heads, hd), row_lse[None], fresh,
    )


def solution(mesh):
    placed = (
        P(("replica", "pool"), "seq", "tensor", None),
        P(("replica", "pool"), None, "seq", "tensor", None),
        P(("replica", "pool"), None, ("tensor", "seq"), None, None),
        P("replica", None, None),
        P("replica"),
        P("replica"),
        P("replica", None, None),
    )
    return jax.shard_map(
        body,
        mesh=mesh,
        in_specs=placed,
        out_specs=(
            P(("replica", "pool"), "seq", "tensor", None),
            P(("replica", "pool"), "tensor", "seq"),
            P(("replica", "pool"), None, ("tensor", "seq"), None, None),
        ),
        check_vma=False,
    )
```

```python
import functools
import math

import jax
import jax.numpy as jnp
from jax import lax
from jax.experimental import pallas as pl
from jax.experimental.pallas import tpu as pltpu
from jax.sharding import PartitionSpec as P

MESH = pl.DeviceIdType.MESH
LOG2E = math.log2(math.e)
LN2 = math.log(2.0)


def kernel(
    sizes, table, prefix, suffix, alloc, q_hbm, sk_hbm, store_ref,
    attn_ref, lse_ref, landed,
    pages, outbox, kv, sfx, freshbox, qin, skin, attn, lse_rows, qf, skf, qb, acc, top, total,
    load_sem, q_sem, sk_sem, attn_sem, lse_sem, own_sem, page_send, page_recv, pass_send, pass_recv,
    sfx_send, sfx_recv, fresh_send, fresh_recv,
):
    n, requests, cap, spages, level_count, heads, kv_all, kv_dev, page, hd = sizes
    rows = page
    group = heads // kv_all
    me = lax.axis_index("pool")
    seq = lax.axis_index("seq")
    other = 1 - seq
    far_right = me < n // 2

    def partner(k):
        high = n - 1 - k
        right = jnp.where(high > me, high, high - 1)
        left = jnp.where(k < me, k, k + 1)
        return jnp.where(far_right, right, left)

    load = pltpu.make_async_copy(store_ref, pages, load_sem)
    load.start()
    q_load = pltpu.make_async_copy(q_hbm, qin, q_sem)
    sk_load = pltpu.make_async_copy(sk_hbm, skin, sk_sem)
    sk_load.start()
    q_load.start()

    barrier = pltpu.get_barrier_semaphore()

    def greet(k, c):
        pl.semaphore_signal(barrier, inc=1, device_id={"pool": partner(k)}, device_id_type=MESH)
        return c

    lax.fori_loop(0, n - 1, greet, 0)
    pl.semaphore_signal(barrier, inc=1, device_id={"seq": other}, device_id_type=MESH)
    pl.semaphore_wait(barrier, n)
    load.wait()

    def slots_of(request):
        live = prefix[request]

        def step(p, state):
            count, picks = state
            mine = (table[request, 0, p] == me) & (p < live)
            slot = table[request, 1, p]
            picks = tuple(
                jnp.where(mine & (count == level), slot, picks[level]) for level in range(level_count)
            )
            return count + mine.astype(jnp.int32), picks

        zero = jnp.int32(0)
        return lax.fori_loop(0, cap, step, (zero, (zero,) * level_count), unroll=cap <= 8)[1]

    def page_copy(k):
        to = partner(k)
        return pltpu.make_async_remote_copy(
            src_ref=outbox.at[to], dst_ref=kv.at[me, seq],
            send_sem=page_send.at[to], recv_sem=page_recv.at[me],
            device_id={"pool": to}, device_id_type=MESH,
        )

    def page_arrival(source):
        return pltpu.make_async_remote_copy(
            src_ref=outbox.at[source], dst_ref=kv.at[source, seq],
            send_sem=page_send.at[source], recv_sem=page_recv.at[source],
            device_id={"pool": source}, device_id_type=MESH,
        )

    def pass_copy(source, half):
        return pltpu.make_async_remote_copy(
            src_ref=kv.at[source, half], dst_ref=kv.at[source, half],
            send_sem=pass_send.at[source], recv_sem=pass_recv.at[source],
            device_id={"seq": other}, device_id_type=MESH,
        )

    def send_pages(k, c):
        to = partner(k)
        picks = slots_of(to)
        for level in range(level_count):
            outbox[to, :, :, level * page:(level + 1) * page, :] = pages[picks[level]]
        page_copy(k).start()
        return c

    lax.fori_loop(0, n // 2, send_pages, 0)

    sk_load.wait()
    skf[...] = skin[...].astype(jnp.float32)
    for a in range(2):
        for h in range(kv_all):
            picked = skf[pl.ds(a * rows * kv_all + h, rows, stride=kv_all), :]
            sfx[seq, a, h] = picked.astype(jnp.bfloat16)

    def sfx_copy(half):
        return pltpu.make_async_remote_copy(
            src_ref=sfx.at[half], dst_ref=sfx.at[half],
            send_sem=sfx_send, recv_sem=sfx_recv,
            device_id={"seq": other}, device_id_type=MESH,
        )

    sfx_copy(seq).start()
    sfx_copy(other).wait_recv()

    def fresh_pick(to):
        pick = jnp.int32(0)
        for q in range(1, spages):
            pick = jnp.where(alloc[q, 0, me] == to, q, pick)
        return sfx[pick, :, pl.ds(seq * kv_dev, kv_dev)]

    def fresh_copy(to, source, at):
        return pltpu.make_async_remote_copy(
            src_ref=freshbox.at[to], dst_ref=landed.at[source],
            send_sem=fresh_send.at[to], recv_sem=fresh_recv.at[source],
            device_id={"pool": at}, device_id_type=MESH,
        )

    def send_fresh(k, c):
        to = partner(k)
        freshbox[to] = fresh_pick(to)
        fresh_copy(to, me, to).start()
        return c

    lax.fori_loop(0, n // 2, send_fresh, 0)
    lax.fori_loop(n // 2, n - 1, send_pages, 0)
    lax.fori_loop(n // 2, n - 1, send_fresh, 0)
    picks = slots_of(me)
    for level in range(level_count):
        kv[me, seq, :, :, level * page:(level + 1) * page, :] = pages[picks[level]]
    pass_copy(me, seq).start()

    freshbox[me] = fresh_pick(me)
    own_fresh = pltpu.make_async_copy(freshbox.at[me], landed.at[me], own_sem)
    own_fresh.start()

    q_load.wait()
    qf[...] = qin[...].astype(jnp.float32)
    for h in range(heads):
        qb[h * rows:(h + 1) * rows, :] = qf[pl.ds(h, rows, stride=heads), :].astype(jnp.bfloat16)

    scale = (hd ** -0.5) * LOG2E

    def attend(j, score_parts, values, biases, first):
        peaks = [jnp.max(part, axis=0, keepdims=True) for part in score_parts]
        peaks = [peak if bias is None else peak + bias for peak, bias in zip(peaks, biases)]
        peak = functools.reduce(jnp.maximum, peaks)
        if not first:
            before = top[j]
            peak = jnp.maximum(before, peak)
        weights = jnp.concatenate([
            jnp.exp2(part - (peak if bias is None else peak - bias))
            for part, bias in zip(score_parts, biases)
        ], axis=0)
        mass = jnp.sum(weights, axis=0, keepdims=True)
        result = lax.dot_general(
            values, weights.astype(jnp.bfloat16), (((0,), (0,)), ((), ())),
            preferred_element_type=jnp.float32,
        )
        if first:
            total[j] = mass
            acc[j] = result
        else:
            fade = jnp.exp2(before - peak)
            total[j] = total[j] * fade + mass
            acc[j] = acc[j] * fade + result
        top[j] = peak

    def score(j, keys):
        return lax.dot_general(
            keys, qb[j * group * rows:(j + 1) * group * rows, :], (((1,), (1,)), ((), ())),
            preferred_element_type=jnp.float32,
        ) * scale

    block = (spages * rows, group * rows)
    token = lax.broadcasted_iota(jnp.int32, block, 1) % rows
    causal = lax.broadcasted_iota(jnp.int32, block, 0) <= token + seq * rows
    for j in range(kv_all):
        keys = sfx[:, 0, j].reshape(spages * rows, hd)
        values = sfx[:, 1, j].reshape(spages * rows, hd)
        attend(j, [jnp.where(causal, score(j, keys), -jnp.inf)], values, [None], True)

    live_mine = prefix[me]

    def attend_source(source):
        def step(p, count):
            hit = (table[me, 0, p] == source) & (p < live_mine)
            return count + hit.astype(jnp.int32)

        count = lax.fori_loop(0, cap, step, jnp.int32(0), unroll=cap <= 8)
        biases = [
            jnp.where(count > level, jnp.float32(0.0), jnp.float32(-jnp.inf))
            for level in range(level_count)
        ]
        for j in range(kv_all):
            scores = score(j, kv[source, j // kv_dev, 0, j % kv_dev])
            parts = [scores[level * page:(level + 1) * page] for level in range(level_count)]
            attend(j, parts, kv[source, j // kv_dev, 1, j % kv_dev], biases, False)

    def relay(k):
        source = partner(k)
        page_arrival(source).wait_recv()
        pass_copy(source, seq).start()

    pass_copy(me, other).wait_recv()
    attend_source(me)
    relay(0)

    def visit(k, c):
        source = partner(k)
        pass_copy(source, other).wait_recv()
        relay(k + 1)
        attend_source(source)
        return c

    lax.fori_loop(0, n - 2, visit, 0)
    pass_copy(partner(n - 2), other).wait_recv()
    attend_source(partner(n - 2))

    suffix_mine = suffix[me]
    ids = lax.broadcasted_iota(jnp.int32, (rows, hd), 0)
    live = ids + seq * rows < suffix_mine * page
    lane = lax.broadcasted_iota(jnp.int32, (1, rows), 1)
    for j in range(kv_all):
        mass = total[j]
        lse = top[j] * LN2 + jnp.log(mass)
        result = acc[j] / mass
        for g in range(group):
            h = j * group + g
            at = slice(g * rows, (g + 1) * rows)
            qf[pl.ds(h, rows, stride=heads), :] = jnp.where(live, result[:, at].T, 0.0)
            lse_rows[h:h + 1, :] = jnp.where(lane + seq * rows < suffix_mine * page, lse[:, at], 0.0)
    attn[...] = qf[...].astype(jnp.bfloat16)
    attn_out = pltpu.make_async_copy(attn, attn_ref, attn_sem)
    lse_out = pltpu.make_async_copy(lse_rows, lse_ref, lse_sem)
    attn_out.start()
    lse_out.start()

    def fresh_wait(k, c):
        source = partner(k)
        fresh_copy(source, source, source).wait_recv()
        return c

    lax.fori_loop(0, n - 1, fresh_wait, 0)
    def drain(k, c):
        to = partner(k)
        page_copy(k).wait_send()
        fresh_copy(to, me, to).wait_send()
        pass_copy(to, seq).wait_send()
        return c

    lax.fori_loop(0, n - 1, drain, 0)
    pass_copy(me, seq).wait_send()
    sfx_copy(seq).wait_send()
    own_fresh.wait()
    attn_out.wait()
    lse_out.wait()


def place(spages, requests, alloc, suffix, attn_in, lse_in, landed, attn_ref, lse_ref, fresh_ref,
          attn, lse, fresh, in_sem, out_sem, fresh_in, fresh_out):
    me = lax.axis_index("pool")
    parts = attn.shape[0]
    attn_loads = [
        pltpu.make_async_copy(attn_in.at[i], attn.at[i], in_sem.at[i]) for i in range(parts)
    ]
    attn_stores = [
        pltpu.make_async_copy(attn.at[i], attn_ref.at[i], out_sem.at[i]) for i in range(parts)
    ]
    lse_load = pltpu.make_async_copy(lse_in, lse, in_sem.at[parts])
    lse_store = pltpu.make_async_copy(lse, lse_ref, out_sem.at[parts])
    for load in attn_loads:
        load.start()
    lse_load.start()
    found = []
    for slot in range(spages):
        def find(r, state):
            source, filled = state
            hit = alloc[slot, 0, r] == me
            alive = hit & (slot < suffix[r])
            return jnp.where(hit, r, source), jnp.where(alive, 1, filled)

        found.append(lax.fori_loop(
            0, requests, find, (jnp.int32(0), jnp.int32(0)), unroll=requests <= 8
        ))
    fresh_loads = [
        pltpu.make_async_copy(landed.at[found[i][0]], fresh.at[i], fresh_in.at[i])
        for i in range(spages)
    ]
    fresh_stores = [
        pltpu.make_async_copy(fresh.at[i], fresh_ref.at[i], fresh_out.at[i])
        for i in range(spages)
    ]
    for load in fresh_loads:
        load.start()
    for load, store in zip(attn_loads, attn_stores):
        load.wait()
        store.start()
    lse_load.wait()
    lse_store.start()
    for slot in range(spages):
        fresh_loads[slot].wait()

        @pl.when(found[slot][1] == 0)
        def _():
            fresh[slot] = jnp.zeros_like(fresh[slot])

        fresh_stores[slot].start()
    for store in attn_stores + [lse_store] + fresh_stores:
        store.wait()


def body(queries, suffix_kv, page_store, holder_table, prefix_pages, suffix_pages, fresh_alloc):
    n = lax.axis_size("pool")
    halves = lax.axis_size("seq")
    slots, _, kv_dev, page, hd = page_store.shape
    requests, cap = holder_table.shape[:2]
    spages = fresh_alloc.shape[1]
    levels = cap // n
    rows, heads = queries.shape[1:3]
    kv_all = suffix_kv.shape[3]
    assert requests == n and rows == page and spages == halves == 2
    assert kv_all == kv_dev * halves
    table = jnp.transpose(holder_table, (0, 2, 1))
    alloc = jnp.transpose(fresh_alloc, (1, 2, 0))
    sizes = (n, requests, cap, spages, levels, heads, kv_all, kv_dev, page, hd)
    bf16, f32 = jnp.bfloat16, jnp.float32
    dma = pltpu.SemaphoreType.DMA
    smem = pl.BlockSpec(memory_space=pltpu.SMEM)
    away = pl.BlockSpec(memory_space=pl.ANY)
    flops = 4 * heads * rows * hd * (cap * page + spages * rows)
    attention, row_lse, landed = pl.pallas_call(
        functools.partial(kernel, sizes),
        out_shape=(
            jax.ShapeDtypeStruct((rows * heads, hd), bf16),
            jax.ShapeDtypeStruct((heads, rows), f32),
            jax.ShapeDtypeStruct((n, 2, kv_dev, page, hd), bf16),
        ),
        in_specs=[smem, smem, smem, smem, away, away, away],
        out_specs=(away, away, away),
        scratch_shapes=[
            pltpu.VMEM((slots, 2, kv_dev, page, hd), bf16),
            pltpu.VMEM((n, 2, kv_dev, levels * page, hd), bf16),
            pltpu.VMEM((n, halves, 2, kv_dev, levels * page, hd), bf16),
            pltpu.VMEM((halves, 2, kv_all, rows, hd), bf16),
            pltpu.VMEM((n, 2, kv_dev, page, hd), bf16),
            pltpu.VMEM((rows * heads, hd), bf16),
            pltpu.VMEM((2 * rows * kv_all, hd), bf16),
            pltpu.VMEM((rows * heads, hd), bf16),
            pltpu.VMEM((heads, rows), f32),
            pltpu.VMEM((rows * heads, hd), f32),
            pltpu.VMEM((2 * rows * kv_all, hd), f32),
            pltpu.VMEM((rows * heads, hd), bf16),
            pltpu.VMEM((kv_all, hd, heads // kv_all * rows), f32),
            pltpu.VMEM((kv_all, 1, heads // kv_all * rows), f32),
            pltpu.VMEM((kv_all, 1, heads // kv_all * rows), f32),
            dma, dma, dma, dma, dma, dma, dma((n,)), dma((n,)), dma((n,)), dma((n,)),
            dma, dma, dma((n,)), dma((n,)),
        ],
        compiler_params=pltpu.CompilerParams(
            collective_id=0, has_side_effects=True, vmem_limit_bytes=58 * 1024 * 1024
        ),
        cost_estimate=pl.CostEstimate(
            flops=flops, bytes_accessed=6 * 1024 * 1024, transcendentals=flops // (4 * hd)
        ),
        name="suffix_attention",
    )(
        table, prefix_pages, suffix_pages, alloc,
        queries.reshape(rows * heads, hd), suffix_kv.reshape(2 * rows * kv_all, hd), page_store,
    )
    parts = 4
    attention, row_lse, fresh = pl.pallas_call(
        functools.partial(place, spages, requests),
        out_shape=(
            jax.ShapeDtypeStruct((parts, rows * heads // parts, hd), bf16),
            jax.ShapeDtypeStruct((heads, rows), f32),
            jax.ShapeDtypeStruct((spages, 2, kv_dev, page, hd), bf16),
        ),
        in_specs=[smem, smem, away, away, away],
        out_specs=(away, away, away),
        scratch_shapes=[
            pltpu.VMEM((parts, rows * heads // parts, hd), bf16),
            pltpu.VMEM((heads, rows), f32),
            pltpu.VMEM((spages, 2, kv_dev, page, hd), bf16),
            dma((parts + 1,)), dma((parts + 1,)), dma((spages,)), dma((spages,)),
        ],
        compiler_params=pltpu.CompilerParams(has_side_effects=True),
        name="place_outputs",
    )(
        alloc, suffix_pages, attention.reshape(parts, rows * heads // parts, hd), row_lse, landed
    )
    return (
        attention.reshape(1, rows, heads, hd), row_lse[None], fresh,
    )


def solution(mesh):
    placed = (
        P(("replica", "pool"), "seq", "tensor", None),
        P(("replica", "pool"), None, "seq", "tensor", None),
        P(("replica", "pool"), None, ("tensor", "seq"), None, None),
        P("replica", None, None),
        P("replica"),
        P("replica"),
        P("replica", None, None),
    )
    return jax.shard_map(
        body,
        mesh=mesh,
        in_specs=placed,
        out_specs=(
            P(("replica", "pool"), "seq", "tensor", None),
            P(("replica", "pool"), "tensor", "seq"),
            P(("replica", "pool"), None, ("tensor", "seq"), None, None),
        ),
        check_vma=False,
    )
```
